32 devices in a mesh: wall: 4 (over y, x), drops: 8 (over z, core).
Axes of the slice: x: 2, y: 2, z: 4, core: 2. Of those that a mesh axis runs over, the one named last changes fastest.
Arguments:
- drop_points: float32 [256, 3, 544], P(('wall', 'drops')), may hold values from -6 to 6
- drop_strength: float32 [256, 3, 544], P(('wall', 'drops')), may hold values from -0.25 to 0.25
- upsample: float32 [544, 2112], replicated, may hold values from -0.25 to 0.25
- base_velocity: float32 [256, 3, 544], P(('wall', 'drops')), may hold values from -6 to 6
- near_drops: int32 [256, 4], P(('wall', 'drops')), may hold values from 0 to 255, as said below
- near_count: int32 [256], P(('wall', 'drops')), may hold values from 2 to 4
- patch_points: float32 [8192, 192], P('wall'), may hold values from -6 to 6
- patch_strength: float32 [8192, 192], P('wall'), may hold values from -1 to 1
- wall_near: int32 [256, 8], P(('wall', 'drops')), may hold values from 0 to 8191
Outputs:
- drop_velocity: float32 [256, 3, 544], P(('wall', 'drops'))
The draws below stay inside these ranges and needn't reach their ends.
Inputs may be any that keep to these rules, and one draw needn't show every extreme that they name: `near_drops`: each entry names a drop of the same drop group (same index along wall). Of the 32 entries of one device, at most 4 name drops of any one device of the group, and on every device some device of the group is named exactly 4 times. Entries at slots k >= near_count are ignored.
All inputs are finite; a program needn't handle non-finite values.
Results may differ from the reference program's by a relative error of at most 0.0003.
Values sent between devices are 32-bit elements; how exact they have to be, the bound alone decides.
A program may use at most 128 MiB of HBM per device.

```python
import math
import jax
import jax.numpy as jnp
import numpy as np
from jax import lax

NC = 544
NU = 2112
PNODES = 64
K_NEAR = 4
K_WALL = 8
DROP_DEV = 8
GROUP_RANKS = 8
WALL_RANKS = 4
DROPS = 256
PATCHES = 8192
CAP = 4


def draw_near_drops(key, part):
    entries = DROP_DEV * K_NEAR
    total_slots = GROUP_RANKS * CAP
    devices = WALL_RANKS * GROUP_RANKS
    keys = jax.random.split(key, devices)

    def one_device(device_key, device):
        first, second, third, fourth = jax.random.split(device_key, 4)
        group = device // GROUP_RANKS
        favored = jax.random.randint(first, (), 0, GROUP_RANKS)
        slot_owner = jnp.arange(total_slots, dtype=jnp.int32) // CAP
        score = jax.random.permutation(second, total_slots).astype(jnp.int32)
        score = jnp.where(slot_owner == favored, score - total_slots, score)
        order = jnp.argsort(score, stable=True)
        owners = slot_owner[order[:entries]]
        owners = owners[jax.random.permutation(third, entries)]
        local = jax.random.randint(fourth, (entries,), 0, DROP_DEV)
        picked = (group * GROUP_RANKS + owners) * DROP_DEV + local
        return picked.astype(jnp.int32).reshape(DROP_DEV, K_NEAR)
    every = jax.vmap(one_device)(keys, jnp.arange(devices, dtype=jnp.int32))
    return every.reshape(DROPS, K_NEAR)


def place_ends(array, own_key, least, high):
    longest = array.shape.index(max(array.shape))
    spots = []
    for shift in (0, 1):
        where = [jax.random.randint(jax.random.fold_in(own_key, axis), (), 0, length) for axis, length in enumerate(array.shape)]
        where[longest] = (where[longest] + shift) % array.shape[longest]
        spots.append(tuple(where))
    return array.at[spots[0]].set(least).at[spots[1]].set(high)


def steps_of(stream_key, extent, pieces, least, top_value):
    def one(dim, shards_of):
        steps = jax.random.uniform(jax.random.fold_in(jax.random.fold_in(stream_key, 6), dim), (shards_of,), jnp.float32, least / len(pieces), top_value / len(pieces))
        return jnp.repeat(jnp.exp(steps), extent[dim] // shards_of).reshape((-1,) + (1,) * (len(extent) - dim - 1))

    factor_of = one(*pieces[0])
    for cut in pieces[1:]:
        factor_of = factor_of * one(*cut)
    return factor_of


def rank_table(amount, skew):
    weights = [(1 << 20) // math.isqrt(grade ** skew) + 1 for grade in range(1, amount + 1)]
    spread = 1 + sum(weights) // (1 << 30)
    return np.cumsum(np.array([max(1, weight // spread) for weight in weights]))


def ranked(rng, shape, amount, lean):
    table = rank_table(amount, lean)
    lot = jax.random.randint(jax.random.fold_in(rng, 1), shape, 0, int(table[amount - 1]))
    grade = jnp.searchsorted(jnp.asarray(table, jnp.int32), lot, side="right")
    return jax.random.permutation(jax.random.fold_in(rng, 2), amount)[grade].astype(jnp.int32)


def normal_values(rng, extent, deviation, most, shards=(), held_as=jnp.bfloat16):
    values = deviation * jax.random.normal(rng, extent, jnp.float32)
    if shards:
        values = values * steps_of(rng, extent, shards, -0.22, 0.18)
    return jnp.clip(values, -most, most).astype(held_as)


def setup_inputs(seed: int = 0) -> dict:
    splits = jax.random.split(jax.random.key(seed), 10)
    return {
        "drop_points": normal_values(splits[0], (DROPS, 3, NC), 1.0, 6.0, ((0, 32),), jnp.float32),
        "drop_strength": normal_values(splits[1], (DROPS, 3, NC), (NU * K_NEAR // 16) ** -0.5, 0.25, ((0, 32),), jnp.float32),
        "upsample": normal_values(splits[2], (NC, NU), NC ** -0.5, 0.25, (), jnp.float32),
        "base_velocity": normal_values(splits[3], (DROPS, 3, NC), 1.0, 6.0, ((0, 32),), jnp.float32),
        "near_drops": draw_near_drops(jax.random.fold_in(splits[9], 71), 0),
        "near_count": place_ends(jax.random.randint(splits[5], (DROPS,), 2, K_NEAR + 1), jax.random.fold_in(splits[5], 1), 2, K_NEAR).astype(jnp.int32),
        "patch_points": normal_values(splits[6], (PATCHES, 3 * PNODES), 1.0, 6.0, ((0, 4),), jnp.float32),
        "patch_strength": normal_values(splits[7], (PATCHES, 3 * PNODES), (PNODES * K_WALL // 16) ** -0.5, 1.0, ((0, 4),), jnp.float32),
        "wall_near": place_ends(ranked(splits[8], (DROPS, K_WALL), PATCHES, 2), jax.random.fold_in(splits[8], 3), 0, PATCHES - 1).astype(jnp.int32),
    }


smoothing_square = 0.25

def stokes_sum(targets, sources, strength):
    delta = targets[:, :, None] - sources[:, None, :]
    dist = lax.optimization_barrier(jnp.sum(delta * delta, axis=0))
    inverse = lax.rsqrt(dist + smoothing_square)
    cubed = inverse * inverse * inverse
    along = lax.optimization_barrier(jnp.sum(delta * strength[:, None, :], axis=0))
    terms = ((dist + 2.0 * smoothing_square) * strength[:, None, :] + along * delta) * cubed
    return lax.optimization_barrier(jnp.sum(terms, axis=2))

def reference(drop_points, drop_strength, upsample, base_velocity, near_drops, near_count, patch_points, patch_strength, wall_near):

    def one_drop(index):
        targets = drop_points[index]
        listed = wall_near[index]
        wall_pts = patch_points[listed].reshape(K_WALL, 3, PNODES).transpose(1, 0, 2).reshape(3, K_WALL * PNODES)
        wall_str = patch_strength[listed].reshape(K_WALL, 3, PNODES).transpose(1, 0, 2).reshape(3, K_WALL * PNODES)
        total = base_velocity[index] + stokes_sum(targets, wall_pts, wall_str)
        for slot in range(K_NEAR):
            partner = near_drops[index, slot]
            coarse_pts = drop_points[partner]
            coarse_str = drop_strength[partner]
            fine_pts = jnp.dot(coarse_pts, upsample, preferred_element_type=jnp.float32, precision=lax.Precision.HIGHEST)
            fine_str = jnp.dot(coarse_str, upsample, preferred_element_type=jnp.float32, precision=lax.Precision.HIGHEST)
            sources = jnp.concatenate([fine_pts, coarse_pts], axis=1)
            strengths = jnp.concatenate([fine_str, -coarse_str], axis=1)
            term = stokes_sum(targets, sources, strengths)
            live = (slot < near_count[index]).astype(jnp.float32)
            total = total + live * term
        return total
    return lax.map(one_drop, jnp.arange(DROPS, dtype=jnp.int32))
```

```python
import functools

import jax
import jax.numpy as jnp
from jax import lax
from jax.experimental import pallas as pl
from jax.experimental.pallas import tpu as pltpu
from jax.sharding import PartitionSpec as P

BF, F32 = jnp.bfloat16, jnp.float32
CHUNK = 512


def pieces(value):
    first = lax.reduce_precision(value, 8, 7)
    rest = value - first
    second = lax.reduce_precision(rest, 8, 7)
    return first, second, lax.reduce_precision(rest - second, 8, 7)


def kernel_pieces(value):
    first = value.astype(BF).astype(F32)
    rest = value - first
    second = rest.astype(BF).astype(F32)
    return first, second, (rest - second).astype(BF).astype(F32)


def target_features(points):
    scaled = 2.0 * points
    norm = pieces(jnp.sum(scaled * scaled, axis=1, keepdims=True) + 1.0)
    coords = pieces(-2.0 * scaled)
    none = jnp.zeros_like(scaled)
    one, zero = jnp.ones_like(norm[0]), jnp.zeros_like(norm[0])
    blocks = [
        (coords[0], norm[0], one),
        (coords[1], norm[1], zero),
        (coords[2], norm[2], zero),
        (coords[0], zero, one),
        (coords[1], zero, zero),
        (coords[2], zero, zero),
        (coords[0], zero, one),
        (coords[1], zero, zero),
    ]
    rows = [part for block in blocks for part in (none,) + block]
    return jnp.concatenate(rows, axis=1).astype(BF).transpose(0, 2, 1)


def pair_kernel(per_drop, counts, src, scale, shift, feat, tgt, base, out, left, right, acc_one, acc_cube):
    width = src.shape[2]
    nodes = feat.shape[1]
    row = lax.broadcasted_iota(jnp.int32, (8, width), 0)

    def block(start, size, features):
        span = pl.ds(start, size)
        dist = jnp.dot(features, left[:, span], preferred_element_type=F32)
        inverse = lax.rsqrt(dist)
        cubed = inverse * inverse * inverse
        coefs = right[:, span]

        def apply(value):
            high = value.astype(BF)
            low = (value - high.astype(F32)).astype(BF)
            dims = (((1,), (1,)), ((), ()))
            return lax.dot_general(high, coefs, dims, preferred_element_type=F32) + lax.dot_general(
                low, coefs, dims, preferred_element_type=F32
            )

        acc_one[...] += apply(inverse)
        acc_cube[...] += apply(cubed)

    def one_drop(i, _):
        acc_one[...] = jnp.zeros_like(acc_one)
        acc_cube[...] = jnp.zeros_like(acc_cube)

        def one_entry(k, _):
            raw = src[i * per_drop + k] * scale[...] + shift[...]
            square = raw * raw
            norm = square[3:4] + square[4:5] + square[5:6]
            values = jnp.where(row == 7, norm, raw)
            first, second, third = kernel_pieces(values)
            left[...] = jnp.concatenate(
                [first, first, first, second, second, second, third, third], axis=0
            ).astype(BF)
            cross = [values * raw[3 + c : 4 + c] for c in range(3)]
            along = cross[0][0:1] + cross[1][1:2] + cross[2][2:3]
            split = [kernel_pieces(part) for part in cross + [values * along]]
            parts = []
            for p, own in enumerate((first, second, third)):
                parts += [own] + [part[p] for part in split]
            parts.append(jnp.zeros_like(first))
            right[...] = jnp.concatenate(parts, axis=0).astype(BF)
            features = feat[i]

            def step(s, _):
                block(pl.multiple_of(s * CHUNK, CHUNK), CHUNK, features)
                return 0

            lax.fori_loop(0, width // CHUNK, step, 0)
            if width % CHUNK:
                block(width - width % CHUNK, width % CHUNK, features)
            return 0

        lax.fori_loop(0, counts[i], one_entry, 0)

        def joined(acc):
            turned = acc[...].T
            return turned[0:40] + turned[40:80] + turned[80:120]

        plain, cube = joined(acc_one), joined(acc_cube)
        x = 2.0 * tgt[i]
        force = cube[0:3]
        scalar = jnp.sum(x * force, axis=0, keepdims=True) - (cube[8:9] + cube[17:18] + cube[26:27])
        total = base[i] + plain[0:3] + force + cube[35:38] + x * scalar
        turned = [jnp.sum(x * cube[8 + 8 * c : 11 + 8 * c], axis=0, keepdims=True) for c in range(3)]
        out[i] = total - jnp.concatenate(turned, axis=0)
        return 0

    lax.fori_loop(0, out.shape[0], one_drop, 0)


def pair_sums(counts, src, scale, shift, feat, tgt, base):
    drops, _, nodes = tgt.shape
    width = src.shape[2]
    per_drop = src.shape[0] // drops
    pairs = src.shape[0] * nodes * width
    vmem = pl.BlockSpec(memory_space=pltpu.VMEM)
    return pl.pallas_call(
        functools.partial(pair_kernel, per_drop),
        out_shape=jax.ShapeDtypeStruct(tgt.shape, F32),
        in_specs=[pl.BlockSpec(memory_space=pltpu.SMEM)] + [vmem] * 6,
        out_specs=vmem,
        scratch_shapes=[
            pltpu.VMEM((64, width), BF),
            pltpu.VMEM((128, width), BF),
            pltpu.VMEM((nodes, 128), F32),
            pltpu.VMEM((nodes, 128), F32),
        ],
        compiler_params=pltpu.CompilerParams(vmem_limit_bytes=40 * 1024 * 1024),
        cost_estimate=pl.CostEstimate(
            flops=pairs * 1200, bytes_accessed=src.size * 4, transcendentals=pairs
        ),
    )(counts, src, scale, shift, feat, tgt, base)


def per_device(
    drop_points,
    drop_strength,
    upsample,
    base_velocity,
    near_drops,
    near_count,
    patch_points,
    patch_strength,
    wall_near,
):
    owned, _, coarse = drop_points.shape
    fine = upsample.shape[1]
    group = lax.axis_size("drops") * owned
    width = -(-(fine + coarse) // 128) * 128

    packed = jnp.concatenate(
        [drop_strength, drop_points, jnp.zeros((owned, 2, coarse), F32)], axis=1
    )
    everyone = lax.all_gather(packed, "drops", axis=0, tiled=True)

    ranks = lax.axis_size("wall")
    held, patch_width = patch_points.shape
    listed = wall_near.shape[1]
    patch_nodes = patch_width // 3
    asked = lax.all_gather(wall_near.reshape(owned * listed), "wall", axis=0, tiled=True)
    mine = asked // held == lax.axis_index("wall")
    spot = jnp.where(mine, asked % held, 0)
    reply = jnp.concatenate(
        [jnp.take(patch_strength, spot, axis=0), jnp.take(patch_points, spot, axis=0)], axis=1
    )
    reply = jnp.where(mine[:, None], reply, 0.0)
    wall = lax.psum_scatter(reply, "wall", scatter_dimension=0, tiled=True)
    wall = wall.reshape(owned, listed, 6, patch_nodes).transpose(0, 2, 1, 3)
    wall = wall.reshape(owned, 6, listed * patch_nodes)
    wall = jnp.concatenate([wall, jnp.zeros((owned, 2, listed * patch_nodes), F32)], axis=1)

    features = target_features(drop_points)
    both = jnp.concatenate(
        [upsample, jnp.eye(coarse, dtype=F32), jnp.zeros((coarse, width - fine - coarse), F32)],
        axis=1,
    )
    entries = jnp.take(everyone, near_drops.reshape(-1) % group, axis=0)
    sources = lax.dot_general(
        entries.reshape(-1, coarse),
        both,
        (((1,), (0,)), ((), ())),
        precision=lax.Precision.HIGHEST,
        preferred_element_type=F32,
    ).reshape(-1, 8, width)

    def scale_of(lanes, plus):
        row = jnp.arange(8, dtype=jnp.int32)[:, None]
        lane = jnp.arange(lanes, dtype=jnp.int32)[None, :]
        sign = jnp.where((row < 3) & (lane >= plus), -2.0, 2.0)
        return jnp.where(row < 6, sign, 0.0).astype(F32), jnp.broadcast_to(
            (row == 6).astype(F32), (8, lanes)
        )

    near = pair_sums(
        near_count, sources, *scale_of(width, fine), features, drop_points, base_velocity
    )
    wall_width = listed * patch_nodes
    return pair_sums(
        jnp.ones((owned,), jnp.int32),
        wall,
        *scale_of(wall_width, wall_width),
        features,
        drop_points,
        near,
    )


def solution(mesh):
    return jax.shard_map(
        per_device,
        mesh=mesh,
        in_specs=(
            P(("wall", "drops"), None, None),
            P(("wall", "drops"), None, None),
            P(),
            P(("wall", "drops"), None, None),
            P(("wall", "drops"), None),
            P(("wall", "drops")),
            P("wall", None),
            P("wall", None),
            P(("wall", "drops"), None),
        ),
        out_specs=P(("wall", "drops"), None, None),
        check_vma=False,
    )
```

```python
import functools

import jax
import jax.numpy as jnp
from jax import lax
from jax.experimental import pallas as pl
from jax.experimental.pallas import tpu as pltpu
from jax.sharding import PartitionSpec as P

BF, F32 = jnp.bfloat16, jnp.float32
CHUNK = 512


def kernel_pieces(value):
    first = value.astype(BF).astype(F32)
    rest = value - first
    second = rest.astype(BF).astype(F32)
    return first, second, (rest - second).astype(BF).astype(F32)


def target_features(packed):
    row = lax.broadcasted_iota(jnp.int32, packed.shape, 0)
    scaled = jnp.where((row >= 3) & (row < 6), 2.0 * packed, 0.0)
    norm = jnp.sum(scaled * scaled, axis=0, keepdims=True) + 1.0
    coords = kernel_pieces(-2.0 * scaled)
    norms = [jnp.where(row == 6, part, 0.0) for part in kernel_pieces(norm)]
    one = jnp.where(row == 7, 1.0, 0.0)
    blocks = [coords[0] + norms[0] + one, coords[1] + norms[1], coords[2] + norms[2]]
    blocks += [coords[0] + one, coords[1], coords[2], coords[0] + one, coords[1]]
    return jnp.concatenate(blocks, axis=0).T.astype(BF)


def pair_kernel(per_drop, counts, *refs):
    count = len(refs) - 11
    src, (scale, shift, tgt, base, out) = refs[:count], refs[count : count + 5]
    left, right, force, feat, acc_one, acc_cube = refs[count + 5 :]
    width = scale.shape[1]
    row = lax.broadcasted_iota(jnp.int32, (8, width), 0)

    def block(start, size):
        span = pl.ds(start, size)
        dist = jnp.dot(feat[...], left[:, span], preferred_element_type=F32)
        inverse = lax.rsqrt(dist)
        cubed = inverse * inverse * inverse
        weights = force[:, span]
        for c in range(3):
            acc_one[c] += sum(
                inverse[:, lane : lane + 128] * weights[c : c + 1, lane : lane + 128]
                for lane in range(0, size, 128)
            )
        high = cubed.astype(BF)
        low = (cubed - high.astype(F32)).astype(BF)
        dims = (((1,), (1,)), ((), ()))
        coefs = right[:, span]
        acc_cube[...] += lax.dot_general(
            high, coefs, dims, preferred_element_type=F32
        ) + lax.dot_general(low, coefs, dims, preferred_element_type=F32)

    def one_drop(i, _):
        acc_one[...] = jnp.zeros_like(acc_one)
        acc_cube[...] = jnp.zeros_like(acc_cube)
        own = tgt[i]
        feat[...] = target_features(own)

        def one_entry(k, _):
            rows = [ref[i * per_drop + k] for ref in src]
            filled = sum(ref.shape[2] for ref in src)
            if filled < width:
                rows.append(jnp.zeros((8, width - filled), F32))
            raw = jnp.concatenate(rows, axis=1) if len(rows) > 1 else rows[0]
            raw = raw * scale[...] + shift[...]
            square = raw * raw
            norm = square[3:4] + square[4:5] + square[5:6]
            values = jnp.where(row == 7, norm, raw)
            force[...] = values
            first, second, third = kernel_pieces(values)
            left[...] = jnp.concatenate(
                [first, first, first, second, second, second, third, third], axis=0
            ).astype(BF)
            cross = [values * raw[3 + c : 4 + c] for c in range(3)]
            along = cross[0][0:1] + cross[1][1:2] + cross[2][2:3]
            split = [kernel_pieces(part) for part in cross + [values * along]]
            parts = []
            for p, whole in enumerate((first, second, third)):
                parts += [whole] + [part[p] for part in split]
            parts.append(jnp.zeros_like(first))
            right[...] = jnp.concatenate(parts, axis=0).astype(BF)

            def step(s, _):
                block(pl.multiple_of(s * CHUNK, CHUNK), CHUNK)
                return 0

            lax.fori_loop(0, width // CHUNK, step, 0)
            if width % CHUNK:
                block(width - width % CHUNK, width % CHUNK)
            return 0

        lax.fori_loop(0, counts[i], one_entry, 0)

        turned = acc_cube[...].T
        cube = turned[0:40] + turned[40:80] + turned[80:120]
        plain = [jnp.sum(acc_one[c].T, axis=0, keepdims=True) for c in range(3)]
        x = 2.0 * own[3:6]
        direct = cube[0:3]
        scalar = jnp.sum(x * direct, axis=0, keepdims=True) - (cube[8:9] + cube[17:18] + cube[26:27])
        total = base[i] + jnp.concatenate(plain, axis=0) + direct + cube[35:38] + x * scalar
        turned = [jnp.sum(x * cube[8 + 8 * c : 11 + 8 * c], axis=0, keepdims=True) for c in range(3)]
        out[i] = total - jnp.concatenate(turned, axis=0)
        return 0

    lax.fori_loop(0, out.shape[0], one_drop, 0)


def pair_sums(counts, src, scale, shift, tgt, base):
    drops, _, nodes = tgt.shape
    width = scale.shape[1]
    per_drop = src[0].shape[0] // drops
    pairs = drops * per_drop * nodes * width
    vmem = pl.BlockSpec(memory_space=pltpu.VMEM)
    return pl.pallas_call(
        functools.partial(pair_kernel, per_drop),
        out_shape=jax.ShapeDtypeStruct(base.shape, F32),
        in_specs=[pl.BlockSpec(memory_space=pltpu.SMEM)] + [vmem] * (len(src) + 4),
        out_specs=vmem,
        scratch_shapes=[
            pltpu.VMEM((64, width), BF),
            pltpu.VMEM((128, width), BF),
            pltpu.VMEM((8, width), F32),
            pltpu.VMEM((nodes, 64), BF),
            pltpu.VMEM((3, nodes, 128), F32),
            pltpu.VMEM((nodes, 128), F32),
        ],
        compiler_params=pltpu.CompilerParams(vmem_limit_bytes=40 * 1024 * 1024),
        cost_estimate=pl.CostEstimate(
            flops=pairs * 800, bytes_accessed=pairs // nodes * 32, transcendentals=pairs
        ),
    )(counts, *src, scale, shift, tgt, base)


def per_device(
    drop_points,
    drop_strength,
    upsample,
    base_velocity,
    near_drops,
    near_count,
    patch_points,
    patch_strength,
    wall_near,
):
    owned, _, coarse = drop_points.shape
    fine = upsample.shape[1]
    group = lax.axis_size("drops") * owned
    width = -(-(fine + coarse) // 128) * 128

    packed = jnp.concatenate(
        [drop_strength, drop_points, jnp.zeros((owned, 2, coarse), F32)], axis=1
    )
    spread = jnp.broadcast_to(packed[None], (group // owned,) + packed.shape)
    everyone = lax.all_to_all(spread, "drops", split_axis=0, concat_axis=0, tiled=True)
    everyone = everyone.reshape(group, 8, coarse)

    ranks = lax.axis_size("wall")
    held, patch_width = patch_points.shape
    listed = wall_near.shape[1]
    patch_nodes = patch_width // 3
    lists = jnp.broadcast_to(wall_near.reshape(1, owned * listed), (ranks, owned * listed))
    asked = lax.all_to_all(lists, "wall", split_axis=0, concat_axis=0, tiled=True).reshape(-1)
    mine = asked // held == lax.axis_index("wall")
    spot = jnp.where(mine, asked % held, 0)
    reply = jnp.concatenate(
        [jnp.take(patch_strength, spot, axis=0), jnp.take(patch_points, spot, axis=0)], axis=1
    )
    reply = jnp.where(mine[:, None], reply, 0.0)
    wall = lax.psum_scatter(reply, "wall", scatter_dimension=0, tiled=True)
    wall = wall.reshape(owned, listed, 6, patch_nodes).transpose(0, 2, 1, 3)
    wall = wall.reshape(owned, 6, listed * patch_nodes)
    wall = jnp.concatenate([wall, jnp.zeros((owned, 2, listed * patch_nodes), F32)], axis=1)

    entries = jnp.take(everyone, near_drops.reshape(-1) % group, axis=0)
    upsampled = lax.dot_general(
        entries.reshape(-1, coarse),
        upsample,
        (((1,), (0,)), ((), ())),
        precision=lax.Precision.HIGH,
        preferred_element_type=F32,
    ).reshape(-1, 8, fine)

    def scale_of(lanes, plus):
        row = jnp.arange(8, dtype=jnp.int32)[:, None]
        lane = jnp.arange(lanes, dtype=jnp.int32)[None, :]
        sign = jnp.where((row < 3) & (lane >= plus), -2.0, 2.0)
        return jnp.where(row < 6, sign, 0.0).astype(F32), jnp.broadcast_to(
            (row == 6).astype(F32), (8, lanes)
        )

    near = pair_sums(
        near_count, (upsampled, entries), *scale_of(width, fine), packed, base_velocity
    )
    wall_width = listed * patch_nodes
    return pair_sums(
        jnp.ones((owned,), jnp.int32),
        (wall,),
        *scale_of(wall_width, wall_width),
        packed,
        near,
    )


def solution(mesh):
    return jax.shard_map(
        per_device,
        mesh=mesh,
        in_specs=(
            P(("wall", "drops"), None, None),
            P(("wall", "drops"), None, None),
            P(),
            P(("wall", "drops"), None, None),
            P(("wall", "drops"), None),
            P(("wall", "drops")),
            P("wall", None),
            P("wall", None),
            P(("wall", "drops"), None),
        ),
        out_specs=P(("wall", "drops"), None, None),
        check_vma=False,
    )
```

```python
import functools

import jax
import jax.numpy as jnp
from jax import lax
from jax.experimental import pallas as pl
from jax.experimental.pallas import tpu as pltpu
from jax.sharding import PartitionSpec as P

BF, F32 = jnp.bfloat16, jnp.float32
CHUNK = 512
GROUP = 16


def kernel_pieces(value):
    first = value.astype(BF).astype(F32)
    rest = value - first
    second = rest.astype(BF).astype(F32)
    return first, second, (rest - second).astype(BF).astype(F32)


def target_features(packed):
    row = lax.broadcasted_iota(jnp.int32, packed.shape, 0)
    scaled = jnp.where((row >= 3) & (row < 6), 2.0 * packed, 0.0)
    norm = jnp.sum(scaled * scaled, axis=0, keepdims=True) + 1.0
    coords = kernel_pieces(-2.0 * scaled)
    norms = [jnp.where(row == 6, part, 0.0) for part in kernel_pieces(norm)]
    one = jnp.where(row == 7, 1.0, 0.0)
    blocks = [coords[0] + norms[0] + one, coords[1] + norms[1], coords[2] + norms[2]]
    blocks += [coords[0] + one, coords[1], coords[2], coords[0] + one, coords[1]]
    return jnp.concatenate(blocks, axis=0).T.astype(BF)


def pair_kernel(per_drop, counts, *refs):
    count = len(refs) - 17
    src, (scale, shift, tgt, base, out) = refs[:count], refs[count : count + 5]
    left, right, force, feat, acc_one, acc_cube = refs[count + 5 : count + 11]
    dist, high, low = (refs[k : k + 2] for k in range(count + 11, count + 17, 2))
    width = scale.shape[1]
    row = lax.broadcasted_iota(jnp.int32, (8, width), 0)

    nodes = feat.shape[0]
    starts = list(range(0, width, CHUNK))
    dims = (((1,), (1,)), ((), ()))

    def distances(n):
        size = min(CHUNK, width - starts[n])
        dist[n % 2][:, :size] = jnp.dot(
            feat[...], left[:, starts[n] : starts[n] + size], preferred_element_type=F32
        )

    def powers(n):
        size = min(CHUNK, width - starts[n])
        lanes = range(0, size, 128)
        weights = [
            [force[c : c + 1, starts[n] + lane : starts[n] + lane + 128] for c in range(3)]
            for lane in lanes
        ]
        for top in range(0, nodes, GROUP):
            rows = slice(top, min(top + GROUP, nodes))
            sums = [acc_one[c, rows] for c in range(3)]
            for weight, lane in zip(weights, lanes):
                inverse = lax.rsqrt(dist[n % 2][rows, lane : lane + 128])
                sums = [part + inverse * weight[c] for c, part in enumerate(sums)]
                cubed = inverse * inverse * inverse
                whole = cubed.astype(BF)
                high[n % 2][rows, lane : lane + 128] = whole
                low[n % 2][rows, lane : lane + 128] = (cubed - whole.astype(F32)).astype(BF)
            for c in range(3):
                acc_one[c, rows] = sums[c]

    def sums(n):
        size = min(CHUNK, width - starts[n])
        coefs = right[:, starts[n] : starts[n] + size]
        acc_cube[...] += lax.dot_general(
            high[n % 2][:, :size], coefs, dims, preferred_element_type=F32
        ) + lax.dot_general(low[n % 2][:, :size], coefs, dims, preferred_element_type=F32)

    def one_drop(i, _):
        acc_one[...] = jnp.zeros_like(acc_one)
        acc_cube[...] = jnp.zeros_like(acc_cube)
        own = tgt[i]
        feat[...] = target_features(own)

        def one_entry(k, _):
            rows = [ref[i * per_drop + k] for ref in src]
            filled = sum(ref.shape[2] for ref in src)
            if filled < width:
                rows.append(jnp.zeros((8, width - filled), F32))
            raw = jnp.concatenate(rows, axis=1) if len(rows) > 1 else rows[0]
            raw = raw * scale[...] + shift[...]
            square = raw * raw
            norm = square[3:4] + square[4:5] + square[5:6]
            values = jnp.where(row == 7, norm, raw)
            force[...] = values
            first, second, third = kernel_pieces(values)
            left[...] = jnp.concatenate(
                [first, first, first, second, second, second, third, third], axis=0
            ).astype(BF)
            cross = [values * raw[3 + c : 4 + c] for c in range(3)]
            along = cross[0][0:1] + cross[1][1:2] + cross[2][2:3]
            split = [kernel_pieces(part) for part in cross + [values * along]]
            parts = []
            for p, whole in enumerate((first, second, third)):
                parts += [whole] + [part[p] for part in split]
            parts.append(jnp.zeros_like(first))
            right[...] = jnp.concatenate(parts, axis=0).astype(BF)

            distances(0)
            for n in range(len(starts)):
                if n + 1 < len(starts):
                    distances(n + 1)
                powers(n)
                sums(n)
            return 0

        lax.fori_loop(0, counts[i], one_entry, 0)

        turned = acc_cube[...].T
        cube = turned[0:40] + turned[40:80] + turned[80:120]
        plain = [jnp.sum(acc_one[c].T, axis=0, keepdims=True) for c in range(3)]
        x = 2.0 * own[3:6]
        direct = cube[0:3]
        scalar = jnp.sum(x * direct, axis=0, keepdims=True) - (cube[8:9] + cube[17:18] + cube[26:27])
        total = base[i] + jnp.concatenate(plain, axis=0) + direct + cube[35:38] + x * scalar
        turned = [jnp.sum(x * cube[8 + 8 * c : 11 + 8 * c], axis=0, keepdims=True) for c in range(3)]
        out[i] = total - jnp.concatenate(turned, axis=0)
        return 0

    lax.fori_loop(0, out.shape[0], one_drop, 0)


def pair_sums(counts, src, scale, shift, tgt, base):
    drops, _, nodes = tgt.shape
    width = scale.shape[1]
    per_drop = src[0].shape[0] // drops
    pairs = drops * per_drop * nodes * width
    vmem = pl.BlockSpec(memory_space=pltpu.VMEM)
    return pl.pallas_call(
        functools.partial(pair_kernel, per_drop),
        out_shape=jax.ShapeDtypeStruct(base.shape, F32),
        in_specs=[pl.BlockSpec(memory_space=pltpu.SMEM)] + [vmem] * (len(src) + 4),
        out_specs=vmem,
        scratch_shapes=[
            pltpu.VMEM((64, width), BF),
            pltpu.VMEM((128, width), BF),
            pltpu.VMEM((8, width), F32),
            pltpu.VMEM((nodes, 64), BF),
            pltpu.VMEM((3, nodes, 128), F32),
            pltpu.VMEM((nodes, 128), F32),
        ]
        + [pltpu.VMEM((nodes, CHUNK), F32)] * 2
        + [pltpu.VMEM((nodes, CHUNK), BF)] * 4,
        compiler_params=pltpu.CompilerParams(vmem_limit_bytes=40 * 1024 * 1024),
        cost_estimate=pl.CostEstimate(
            flops=pairs * 4000, bytes_accessed=pairs // nodes * 32, transcendentals=pairs
        ),
    )(counts, *src, scale, shift, tgt, base)


def per_device(
    drop_points,
    drop_strength,
    upsample,
    base_velocity,
    near_drops,
    near_count,
    patch_points,
    patch_strength,
    wall_near,
):
    owned, _, coarse = drop_points.shape
    fine = upsample.shape[1]
    group = lax.axis_size("drops") * owned
    width = -(-(fine + coarse) // 128) * 128

    packed = jnp.concatenate(
        [drop_strength, drop_points, jnp.zeros((owned, 2, coarse), F32)], axis=1
    )
    spread = jnp.broadcast_to(packed[None], (group // owned,) + packed.shape)
    everyone = lax.all_to_all(spread, "drops", split_axis=0, concat_axis=0, tiled=True)
    everyone = everyone.reshape(group, 8, coarse)

    ranks = lax.axis_size("wall")
    held, patch_width = patch_points.shape
    listed = wall_near.shape[1]
    patch_nodes = patch_width // 3
    lists = jnp.broadcast_to(wall_near.reshape(1, owned * listed), (ranks, owned * listed))
    asked = lax.all_to_all(lists, "wall", split_axis=0, concat_axis=0, tiled=True).reshape(-1)
    mine = asked // held == lax.axis_index("wall")
    spot = jnp.where(mine, asked % held, 0)
    reply = jnp.concatenate(
        [jnp.take(patch_strength, spot, axis=0), jnp.take(patch_points, spot, axis=0)], axis=1
    )
    reply = jnp.where(mine[:, None], reply, 0.0)
    wall = lax.psum_scatter(reply, "wall", scatter_dimension=0, tiled=True)
    entries = jnp.take(everyone, near_drops.reshape(-1) % group, axis=0)
    upsampled = lax.dot_general(
        entries.reshape(-1, coarse),
        upsample,
        (((1,), (0,)), ((), ())),
        precision=lax.Precision.HIGH,
        preferred_element_type=F32,
    ).reshape(-1, 8, fine)

    def scale_of(lanes, plus):
        row = jnp.arange(8, dtype=jnp.int32)[:, None]
        lane = jnp.arange(lanes, dtype=jnp.int32)[None, :]
        sign = jnp.where((row < 3) & (lane >= plus), -2.0, 2.0)
        return jnp.where(row < 6, sign, 0.0).astype(F32), jnp.broadcast_to(
            (row == 6).astype(F32), (8, lanes)
        )

    near = pair_sums(
        near_count, (upsampled, entries), *scale_of(width, fine), packed, base_velocity
    )
    wall, near = lax.optimization_barrier((wall, near))
    wall = wall.reshape(owned, listed, 6, patch_nodes).transpose(0, 2, 1, 3)
    wall = wall.reshape(owned, 6, listed * patch_nodes)
    wall = jnp.concatenate([wall, jnp.zeros((owned, 2, listed * patch_nodes), F32)], axis=1)
    wall_width = listed * patch_nodes
    return pair_sums(
        jnp.ones((owned,), jnp.int32),
        (wall,),
        *scale_of(wall_width, wall_width),
        packed,
        near,
    )


def solution(mesh):
    return jax.shard_map(
        per_device,
        mesh=mesh,
        in_specs=(
            P(("wall", "drops"), None, None),
            P(("wall", "drops"), None, None),
            P(),
            P(("wall", "drops"), None, None),
            P(("wall", "drops"), None),
            P(("wall", "drops")),
            P("wall", None),
            P("wall", None),
            P(("wall", "drops"), None),
        ),
        out_specs=P(("wall", "drops"), None, None),
        check_vma=False,
    )
```

```python
import functools

import jax
import jax.numpy as jnp
from jax import lax
from jax.experimental import pallas as pl
from jax.experimental.pallas import tpu as pltpu
from jax.sharding import PartitionSpec as P

BF, F32 = jnp.bfloat16, jnp.float32
CHUNK = 512
GROUP = 16


def kernel_pieces(value):
    first = value.astype(BF).astype(F32)
    rest = value - first
    second = rest.astype(BF).astype(F32)
    return first, second, (rest - second).astype(BF).astype(F32)


def target_features(packed):
    row = lax.broadcasted_iota(jnp.int32, packed.shape, 0)
    scaled = jnp.where((row >= 3) & (row < 6), 2.0 * packed, 0.0)
    norm = jnp.sum(scaled * scaled, axis=0, keepdims=True) + 1.0
    coords = kernel_pieces(-2.0 * scaled)
    norms = [jnp.where(row == 6, part, 0.0) for part in kernel_pieces(norm)]
    one = jnp.where(row == 7, 1.0, 0.0)
    blocks = [coords[0] + norms[0] + one, coords[1] + norms[1], coords[2] + norms[2]]
    blocks += [coords[0] + one, coords[1], coords[2], coords[0] + one, coords[1]]
    return jnp.concatenate(blocks, axis=0).T.astype(BF)


def pair_kernel(per_drop, counts, *refs):
    count = len(refs) - 15
    src, (scale, shift, tgt, base, out) = refs[:count], refs[count : count + 5]
    left, right, force, feat, acc_one, acc_cube = refs[count + 5 : count + 11]
    dist, split = refs[count + 11 : count + 13], refs[count + 13 :]
    width = scale.shape[1]
    row = lax.broadcasted_iota(jnp.int32, (8, width), 0)

    nodes = feat.shape[0]
    starts = list(range(0, width, CHUNK))

    def distances(n):
        size = min(CHUNK, width - starts[n])
        dist[n % 2][:, :size] = jnp.dot(
            feat[...], left[:, starts[n] : starts[n] + size], preferred_element_type=F32
        )

    def powers(n):
        size = min(CHUNK, width - starts[n])
        lanes = range(0, size, 128)
        weights = [
            [force[c : c + 1, starts[n] + lane : starts[n] + lane + 128] for c in range(3)]
            for lane in lanes
        ]
        for top in range(0, nodes, GROUP):
            rows = slice(top, min(top + GROUP, nodes))
            below = slice(nodes + rows.start, nodes + rows.stop)
            sums = [acc_one[c, rows] for c in range(3)]
            for weight, lane in zip(weights, lanes):
                inverse = lax.rsqrt(dist[n % 2][rows, lane : lane + 128])
                sums = [part + inverse * weight[c] for c, part in enumerate(sums)]
                cubed = inverse * inverse * inverse
                whole = cubed.astype(BF)
                split[n % 2][rows, lane : lane + 128] = whole
                split[n % 2][below, lane : lane + 128] = (cubed - whole.astype(F32)).astype(BF)
            for c in range(3):
                acc_one[c, rows] = sums[c]

    def sums(n):
        size = min(CHUNK, width - starts[n])
        acc_cube[...] += jnp.dot(
            split[n % 2][:, :size],
            right[starts[n] : starts[n] + size],
            preferred_element_type=F32,
        )

    def one_drop(i, _):
        acc_one[...] = jnp.zeros_like(acc_one)
        acc_cube[...] = jnp.zeros_like(acc_cube)
        own = tgt[i]
        feat[...] = target_features(own)

        def one_entry(k, _):
            rows = [ref[i * per_drop + k] for ref in src]
            filled = sum(ref.shape[2] for ref in src)
            if filled < width:
                rows.append(jnp.zeros((8, width - filled), F32))
            raw = jnp.concatenate(rows, axis=1) if len(rows) > 1 else rows[0]
            raw = raw * scale[...] + shift[...]
            square = raw * raw
            norm = square[3:4] + square[4:5] + square[5:6]
            values = jnp.where(row == 7, norm, raw)
            force[...] = values
            first, second, third = kernel_pieces(values)
            left[...] = jnp.concatenate(
                [first, first, first, second, second, second, third, third], axis=0
            ).astype(BF)
            cross = [values * raw[3 + c : 4 + c] for c in range(3)]
            along = cross[0][0:1] + cross[1][1:2] + cross[2][2:3]
            shares = [kernel_pieces(part) for part in cross + [values * along]]
            parts = []
            for p, whole in enumerate((first, second, third)):
                parts += [whole] + [part[p] for part in shares]
            parts.append(jnp.zeros_like(first))
            right[...] = jnp.concatenate(parts, axis=0).T.astype(BF)

            distances(0)
            for n in range(len(starts)):
                if n + 1 < len(starts):
                    distances(n + 1)
                powers(n)
                sums(n)
            return 0

        lax.fori_loop(0, counts[i], one_entry, 0)

        turned = (acc_cube[:nodes] + acc_cube[nodes:]).T
        cube = turned[0:40] + turned[40:80] + turned[80:120]
        plain = [jnp.sum(acc_one[c].T, axis=0, keepdims=True) for c in range(3)]
        x = 2.0 * own[3:6]
        direct = cube[0:3]
        scalar = jnp.sum(x * direct, axis=0, keepdims=True) - (cube[8:9] + cube[17:18] + cube[26:27])
        total = base[i] + jnp.concatenate(plain, axis=0) + direct + cube[35:38] + x * scalar
        turned = [jnp.sum(x * cube[8 + 8 * c : 11 + 8 * c], axis=0, keepdims=True) for c in range(3)]
        out[i] = total - jnp.concatenate(turned, axis=0)
        return 0

    lax.fori_loop(0, out.shape[0], one_drop, 0)


def pair_sums(counts, src, scale, shift, tgt, base):
    drops, _, nodes = tgt.shape
    width = scale.shape[1]
    per_drop = src[0].shape[0] // drops
    pairs = drops * per_drop * nodes * width
    vmem = pl.BlockSpec(memory_space=pltpu.VMEM)
    return pl.pallas_call(
        functools.partial(pair_kernel, per_drop),
        out_shape=jax.ShapeDtypeStruct(base.shape, F32),
        in_specs=[pl.BlockSpec(memory_space=pltpu.SMEM)] + [vmem] * (len(src) + 4),
        out_specs=vmem,
        scratch_shapes=[
            pltpu.VMEM((64, width), BF),
            pltpu.VMEM((width, 128), BF),
            pltpu.VMEM((8, width), F32),
            pltpu.VMEM((nodes, 64), BF),
            pltpu.VMEM((3, nodes, 128), F32),
            pltpu.VMEM((2 * nodes, 128), F32),
        ]
        + [pltpu.VMEM((nodes, CHUNK), F32)] * 2
        + [pltpu.VMEM((2 * nodes, CHUNK), BF)] * 2,
        compiler_params=pltpu.CompilerParams(vmem_limit_bytes=40 * 1024 * 1024),
        cost_estimate=pl.CostEstimate(
            flops=pairs * 4000, bytes_accessed=pairs // nodes * 32, transcendentals=pairs
        ),
    )(counts, *src, scale, shift, tgt, base)


def scale_of(lanes, plus):
    row = jnp.arange(8, dtype=jnp.int32)[:, None]
    lane = jnp.arange(lanes, dtype=jnp.int32)[None, :]
    sign = jnp.where((row < 3) & (lane >= plus), -2.0, 2.0)
    return jnp.where(row < 6, sign, 0.0).astype(F32), jnp.broadcast_to(
        (row == 6).astype(F32), (8, lanes)
    )


def per_device(
    drop_points,
    drop_strength,
    upsample,
    base_velocity,
    near_drops,
    near_count,
    patch_points,
    patch_strength,
    wall_near,
):
    owned, _, coarse = drop_points.shape
    fine = upsample.shape[1]
    group = lax.axis_size("drops") * owned
    width = -(-(fine + coarse) // 128) * 128

    packed = jnp.concatenate(
        [drop_strength, drop_points, jnp.zeros((owned, 2, coarse), F32)], axis=1
    )
    flat = packed[:, :6].reshape(1, owned, 6 * coarse)
    spread = jnp.broadcast_to(flat, (group // owned,) + flat.shape[1:])
    everyone = lax.all_to_all(spread, "drops", split_axis=0, concat_axis=0, tiled=True)
    everyone = everyone.reshape(group, 6 * coarse)

    ranks = lax.axis_size("wall")
    held, patch_width = patch_points.shape
    listed = wall_near.shape[1]
    patch_nodes = patch_width // 3
    lists = jnp.broadcast_to(wall_near.reshape(1, owned * listed), (ranks, owned * listed))
    asked = lax.all_to_all(lists, "wall", split_axis=0, concat_axis=0, tiled=True).reshape(-1)
    mine = asked // held == lax.axis_index("wall")
    spot = jnp.where(mine, asked % held, 0)
    reply = jnp.concatenate(
        [jnp.take(patch_strength, spot, axis=0), jnp.take(patch_points, spot, axis=0)], axis=1
    )
    reply = jnp.where(mine[:, None], reply, 0.0)
    reply = reply.reshape(ranks, owned * listed, 2 * patch_width)
    back = lax.all_to_all(reply, "wall", split_axis=0, concat_axis=0, tiled=True)
    wall = jnp.sum(back, axis=0)
    wall = wall.reshape(owned, listed, 6, patch_nodes).transpose(0, 2, 1, 3)
    wall = wall.reshape(owned, 6, listed * patch_nodes)
    wall = jnp.concatenate([wall, jnp.zeros((owned, 2, listed * patch_nodes), F32)], axis=1)
    wall_width = listed * patch_nodes
    total = pair_sums(
        jnp.ones((owned,), jnp.int32), (wall,), *scale_of(wall_width, wall_width), packed, base_velocity
    )

    everyone, total = lax.optimization_barrier((everyone, total))
    entries = jnp.take(everyone, near_drops.reshape(-1) % group, axis=0).reshape(-1, 6, coarse)
    entries = jnp.concatenate([entries, jnp.zeros((entries.shape[0], 2, coarse), F32)], axis=1)
    upsampled = lax.dot_general(
        entries.reshape(-1, coarse),
        upsample,
        (((1,), (0,)), ((), ())),
        precision=lax.Precision.HIGH,
        preferred_element_type=F32,
    ).reshape(-1, 8, fine)

    return pair_sums(near_count, (upsampled, entries), *scale_of(width, fine), packed, total)


def solution(mesh):
    return jax.shard_map(
        per_device,
        mesh=mesh,
        in_specs=(
            P(("wall", "drops"), None, None),
            P(("wall", "drops"), None, None),
            P(),
            P(("wall", "drops"), None, None),
            P(("wall", "drops"), None),
            P(("wall", "drops")),
            P("wall", None),
            P("wall", None),
            P(("wall", "drops"), None),
        ),
        out_specs=P(("wall", "drops"), None, None),
        check_vma=False,
    )
```

```python
import functools

import jax
import jax.numpy as jnp
from jax import lax
from jax.experimental import pallas as pl
from jax.experimental.pallas import tpu as pltpu
from jax.sharding import PartitionSpec as P

BF, F32 = jnp.bfloat16, jnp.float32
CHUNK = 1024
GROUP = 16


def kernel_pieces(value):
    first = value.astype(BF).astype(F32)
    rest = value - first
    second = rest.astype(BF).astype(F32)
    return first, second, (rest - second).astype(BF).astype(F32)


def target_features(packed):
    row = lax.broadcasted_iota(jnp.int32, packed.shape, 0)
    scaled = jnp.where((row >= 3) & (row < 6), 2.0 * packed, 0.0)
    norm = jnp.sum(scaled * scaled, axis=0, keepdims=True) + 1.0
    coords = kernel_pieces(-2.0 * scaled)
    norms = [jnp.where(row == 6, part, 0.0) for part in kernel_pieces(norm)]
    one = jnp.where(row == 7, 1.0, 0.0)
    blocks = [coords[0] + norms[0] + one, coords[1] + norms[1], coords[2] + norms[2]]
    blocks += [coords[0] + one, coords[1], coords[2], coords[0] + one, coords[1]]
    return jnp.concatenate(blocks, axis=0).T.astype(BF)


def pair_kernel(per_drop, counts, *refs):
    count = len(refs) - 15
    src, (scale, shift, tgt, base, out) = refs[:count], refs[count : count + 5]
    left, right, force, feat, acc_one, acc_cube = refs[count + 5 : count + 11]
    dist, split = refs[count + 11 : count + 13], refs[count + 13 :]
    width = scale.shape[1]
    row = lax.broadcasted_iota(jnp.int32, (8, width), 0)

    nodes = feat.shape[0]
    starts = list(range(0, width, CHUNK))

    def distances(n):
        size = min(CHUNK, width - starts[n])
        dist[n % 2][:, :size] = jnp.dot(
            feat[...], left[:, starts[n] : starts[n] + size], preferred_element_type=F32
        )

    def powers(n):
        size = min(CHUNK, width - starts[n])
        lanes = range(0, size, 128)
        weights = [
            [force[c : c + 1, starts[n] + lane : starts[n] + lane + 128] for c in range(3)]
            for lane in lanes
        ]
        for top in range(0, nodes, GROUP):
            rows = slice(top, min(top + GROUP, nodes))
            below = slice(nodes + rows.start, nodes + rows.stop)
            sums = [acc_one[c, rows] for c in range(3)]
            for weight, lane in zip(weights, lanes):
                inverse = lax.rsqrt(dist[n % 2][rows, lane : lane + 128])
                sums = [part + inverse * weight[c] for c, part in enumerate(sums)]
                cubed = inverse * inverse * inverse
                whole = cubed.astype(BF)
                split[n % 2][rows, lane : lane + 128] = whole
                split[n % 2][below, lane : lane + 128] = (cubed - whole.astype(F32)).astype(BF)
            for c in range(3):
                acc_one[c, rows] = sums[c]

    def sums(n):
        size = min(CHUNK, width - starts[n])
        acc_cube[...] += jnp.dot(
            split[n % 2][:, :size],
            right[starts[n] : starts[n] + size],
            preferred_element_type=F32,
        )

    def one_drop(i, _):
        acc_one[...] = jnp.zeros_like(acc_one)
        acc_cube[...] = jnp.zeros_like(acc_cube)
        own = tgt[i]
        feat[...] = target_features(own)

        def one_entry(k, _):
            rows = [ref[i * per_drop + k] for ref in src]
            filled = sum(ref.shape[2] for ref in src)
            if filled < width:
                rows.append(jnp.zeros((8, width - filled), F32))
            raw = jnp.concatenate(rows, axis=1) if len(rows) > 1 else rows[0]
            raw = raw * scale[...] + shift[...]
            square = raw * raw
            norm = square[3:4] + square[4:5] + square[5:6]
            values = jnp.where(row == 7, norm, raw)
            force[...] = values
            first, second, third = kernel_pieces(values)
            left[...] = jnp.concatenate(
                [first, first, first, second, second, second, third, third], axis=0
            ).astype(BF)
            cross = [values * raw[3 + c : 4 + c] for c in range(3)]
            along = cross[0][0:1] + cross[1][1:2] + cross[2][2:3]
            shares = [kernel_pieces(part) for part in cross + [values * along]]
            parts = []
            for p, whole in enumerate((first, second, third)):
                parts += [whole] + [part[p] for part in shares]
            parts.append(jnp.zeros_like(first))
            right[...] = jnp.concatenate(parts, axis=0).T.astype(BF)

            distances(0)
            for n in range(len(starts)):
                if n + 1 < len(starts):
                    distances(n + 1)
                powers(n)
                sums(n)
            return 0

        lax.fori_loop(0, counts[i], one_entry, 0)

        turned = (acc_cube[:nodes] + acc_cube[nodes:]).T
        cube = turned[0:40] + turned[40:80] + turned[80:120]
        plain = [jnp.sum(acc_one[c].T, axis=0, keepdims=True) for c in range(3)]
        x = 2.0 * own[3:6]
        direct = cube[0:3]
        scalar = jnp.sum(x * direct, axis=0, keepdims=True) - (cube[8:9] + cube[17:18] + cube[26:27])
        total = base[i] + jnp.concatenate(plain, axis=0) + direct + cube[35:38] + x * scalar
        turned = [jnp.sum(x * cube[8 + 8 * c : 11 + 8 * c], axis=0, keepdims=True) for c in range(3)]
        out[i] = total - jnp.concatenate(turned, axis=0)
        return 0

    lax.fori_loop(0, out.shape[0], one_drop, 0)


def pair_sums(counts, src, scale, shift, tgt, base):
    drops, _, nodes = tgt.shape
    width = scale.shape[1]
    per_drop = src[0].shape[0] // drops
    pairs = drops * per_drop * nodes * width
    vmem = pl.BlockSpec(memory_space=pltpu.VMEM)
    return pl.pallas_call(
        functools.partial(pair_kernel, per_drop),
        out_shape=jax.ShapeDtypeStruct(base.shape, F32),
        in_specs=[pl.BlockSpec(memory_space=pltpu.SMEM)] + [vmem] * (len(src) + 4),
        out_specs=vmem,
        scratch_shapes=[
            pltpu.VMEM((64, width), BF),
            pltpu.VMEM((width, 128), BF),
            pltpu.VMEM((8, width), F32),
            pltpu.VMEM((nodes, 64), BF),
            pltpu.VMEM((3, nodes, 128), F32),
            pltpu.VMEM((2 * nodes, 128), F32),
        ]
        + [pltpu.VMEM((nodes, CHUNK), F32)] * 2
        + [pltpu.VMEM((2 * nodes, CHUNK), BF)] * 2,
        compiler_params=pltpu.CompilerParams(vmem_limit_bytes=40 * 1024 * 1024),
        cost_estimate=pl.CostEstimate(
            flops=pairs * 4000, bytes_accessed=pairs // nodes * 32, transcendentals=pairs
        ),
    )(counts, *src, scale, shift, tgt, base)


def scale_of(lanes, plus):
    row = jnp.arange(8, dtype=jnp.int32)[:, None]
    lane = jnp.arange(lanes, dtype=jnp.int32)[None, :]
    sign = jnp.where((row < 3) & (lane >= plus), -2.0, 2.0)
    return jnp.where(row < 6, sign, 0.0).astype(F32), jnp.broadcast_to(
        (row == 6).astype(F32), (8, lanes)
    )


def per_device(
    drop_points,
    drop_strength,
    upsample,
    base_velocity,
    near_drops,
    near_count,
    patch_points,
    patch_strength,
    wall_near,
):
    owned, _, coarse = drop_points.shape
    fine = upsample.shape[1]
    group = lax.axis_size("drops") * owned
    width = -(-(fine + coarse) // 128) * 128

    packed = jnp.concatenate(
        [drop_strength, drop_points, jnp.zeros((owned, 2, coarse), F32)], axis=1
    )
    flat = packed[:, :6].reshape(1, owned, 6 * coarse)
    spread = jnp.broadcast_to(flat, (group // owned,) + flat.shape[1:])
    everyone = lax.all_to_all(spread, "drops", split_axis=0, concat_axis=0, tiled=True)
    everyone = everyone.reshape(group, 6 * coarse)

    ranks = lax.axis_size("wall")
    held, patch_width = patch_points.shape
    listed = wall_near.shape[1]
    patch_nodes = patch_width // 3
    lists = jnp.broadcast_to(wall_near.reshape(1, owned * listed), (ranks, owned * listed))
    asked = lax.all_to_all(lists, "wall", split_axis=0, concat_axis=0, tiled=True).reshape(-1)
    mine = asked // held == lax.axis_index("wall")
    spot = jnp.where(mine, asked % held, 0)
    reply = jnp.concatenate(
        [jnp.take(patch_strength, spot, axis=0), jnp.take(patch_points, spot, axis=0)], axis=1
    )
    reply = jnp.where(mine[:, None], reply, 0.0)
    reply = reply.reshape(ranks, owned * listed, 2 * patch_width)
    back = lax.all_to_all(reply, "wall", split_axis=0, concat_axis=0, tiled=True)
    wall = jnp.sum(back, axis=0)
    wall = wall.reshape(owned, listed, 6, patch_nodes).transpose(0, 2, 1, 3)
    wall = wall.reshape(owned, 6, listed * patch_nodes)
    wall = jnp.concatenate([wall, jnp.zeros((owned, 2, listed * patch_nodes), F32)], axis=1)
    wall_width = listed * patch_nodes
    total = pair_sums(
        jnp.ones((owned,), jnp.int32), (wall,), *scale_of(wall_width, wall_width), packed, base_velocity
    )

    everyone, total = lax.optimization_barrier((everyone, total))
    entries = jnp.take(everyone, near_drops.reshape(-1) % group, axis=0).reshape(-1, 6, coarse)
    entries = jnp.concatenate([entries, jnp.zeros((entries.shape[0], 2, coarse), F32)], axis=1)
    upsampled = lax.dot_general(
        entries.reshape(-1, coarse),
        upsample,
        (((1,), (0,)), ((), ())),
        precision=lax.Precision.HIGH,
        preferred_element_type=F32,
    ).reshape(-1, 8, fine)

    return pair_sums(near_count, (upsampled, entries), *scale_of(width, fine), packed, total)


def solution(mesh):
    return jax.shard_map(
        per_device,
        mesh=mesh,
        in_specs=(
            P(("wall", "drops"), None, None),
            P(("wall", "drops"), None, None),
            P(),
            P(("wall", "drops"), None, None),
            P(("wall", "drops"), None),
            P(("wall", "drops")),
            P("wall", None),
            P("wall", None),
            P(("wall", "drops"), None),
        ),
        out_specs=P(("wall", "drops"), None, None),
        check_vma=False,
    )
```
